32 devices in a mesh: sample: 4 (over z), sect: 4 (over x, core), dom: 2 (over y).
Axes of the slice: x: 2, y: 2, z: 4, core: 2. Of those that a mesh axis runs over, the one named last changes fastest.
Arguments:
- features: bfloat16 [8, 512, 512], P(('sample', 'dom'), 'sect'), may hold values from -6 to 6
- weight: bfloat16 [4608, 512], P('sample', 'sect'), may hold values from -0.09375 to 0.09375
- style: float32 [8, 512], P(('sample', 'dom')), may hold values from 0.3 to 3
- bias: float32 [512], P('sect'), may hold values from -3 to 3
- adjoint: bfloat16 [8, 512, 512], P(('sample', 'dom'), 'sect'), may hold values from -6 to 6
Outputs:
- styled: bfloat16 [8, 512, 512], P(('sample', 'dom'), 'sect')
- grad_weight: float32 [4608, 512], P(('sample', 'dom'), 'sect')
- grad_features: bfloat16 [8, 512, 512], P(('sample', 'dom'), 'sect')
The draws below stay inside these ranges and needn't reach their ends.
All inputs are finite; a program needn't handle non-finite values.
Results may differ from the reference program's by a relative error of at most 0.0049.
Values may be sent and summed in bfloat16 or wider, within the bound.
A program may use at most 64 MiB of HBM per device.

```python
import math
import jax
import jax.numpy as jnp
from jax import lax

CH = 512
WIDTH = 64
ROWS = 8
BATCH = 8


def level_of(own_key, shape, split, low, largest):
    loudness = 1.0
    for axis_at, shards_of in split:
        draws = jax.random.uniform(jax.random.fold_in(jax.random.fold_in(own_key, 6), axis_at), (shards_of,), jnp.float32, low / len(split), largest / len(split))
        loudness = loudness * jnp.repeat(jnp.exp(draws), shape[axis_at] // shards_of).reshape((-1,) + (1,) * (len(shape) - 1 - axis_at))
    return loudness


def scatter_about(own_key, shape, scale, limit, cuts=(), dtype=jnp.bfloat16):
    values = jax.random.normal(own_key, shape, jnp.float32) * scale
    if len(cuts) > 0:
        values = level_of(own_key, shape, cuts, -0.22, 0.18) * values
    return jnp.clip(values, min=-limit, max=limit).astype(dtype)


def setup_inputs(seed: int = 0) -> dict:
    streams_of = jax.random.split(jax.random.key(seed), 6)
    return {
        "features": scatter_about(streams_of[0], (BATCH, CH, ROWS * WIDTH), 1.0, 6.0, ((0, 8), (1, 4))),
        "weight": scatter_about(streams_of[1], (9 * CH, CH), (9 * CH) ** -0.5, 0.09375, ((0, 4), (1, 4))),
        "style": jnp.clip(jnp.exp(math.log(3.0) - 2.3025851 * jax.random.uniform(streams_of[2], (BATCH, CH), jnp.float32) ** level_of(streams_of[2], (BATCH, CH), ((0, 8),), -0.2, 0.2)), 0.3, 3.0),
        "bias": scatter_about(streams_of[3], (CH,), 0.5, 3.0, ((0, 4),), jnp.float32),
        "adjoint": scatter_about(streams_of[4], (BATCH, CH, ROWS * WIDTH), 1.0, 6.0, ((0, 8), (1, 4))),
    }


OFFSETS = [(-1, -1), (-1, 0), (-1, 1), (0, -1), (0, 0), (0, 1), (1, -1), (1, 0), (1, 1)]
EPSILON = 1e-08

def moved(array, row_step, col_step):
    count = array.shape[0]
    depth = array.shape[1]
    grid = array.reshape(count, depth, ROWS, WIDTH)
    padded = jnp.pad(grid, ((0, 0), (0, 0), (1, 1), (1, 1)))
    part = padded[:, :, 1 + row_step:1 + row_step + ROWS, 1 + col_step:1 + col_step + WIDTH]
    return part.reshape(count, depth, ROWS * WIDTH)

def reference(features, weight, style, bias, adjoint):
    channels = features.shape[1]
    modulated = (features.astype(jnp.float32) * style[:, :, None]).astype(jnp.bfloat16)
    kernel = weight.reshape(9, channels, channels)
    kernel_f = kernel.astype(jnp.float32)
    shifts = [moved(modulated, row_step, col_step).astype(jnp.float32) for row_step, col_step in OFFSETS]
    conv_out = jnp.zeros(features.shape, jnp.float32)
    for index in range(9):
        conv_out = conv_out + jnp.einsum('nip,io->nop', shifts[index], kernel_f[index])
    kernel_sq = lax.optimization_barrier(jnp.sum(kernel_f * kernel_f, axis=0))
    style_sq = style * style
    energy = jnp.dot(style_sq, kernel_sq, precision=lax.Precision.HIGHEST) + EPSILON
    demod = lax.rsqrt(energy)
    styled = (conv_out * demod[:, :, None] + bias[None, :, None]).astype(jnp.bfloat16)
    adjoint_f = adjoint.astype(jnp.float32)
    scaled_adjoint = (adjoint_f * demod[:, :, None]).astype(jnp.bfloat16)
    scaled_f = scaled_adjoint.astype(jnp.float32)
    demod_grad = lax.optimization_barrier(jnp.sum(adjoint_f * conv_out, axis=2))
    energy_grad = -0.5 * demod_grad * demod * demod * demod
    coupling = jnp.dot(style_sq.T, energy_grad, precision=lax.Precision.HIGHEST)
    grads = []
    back = jnp.zeros(features.shape, jnp.float32)
    for index in range(9):
        row_step, col_step = OFFSETS[index]
        grads.append(jnp.einsum('nip,nop->io', shifts[index], scaled_f) + 2.0 * kernel_f[index] * coupling)
        partial_back = jnp.einsum('nop,io->nip', scaled_f, kernel_f[index])
        back = back + moved(partial_back, -row_step, -col_step)
    grad_weight = jnp.concatenate(grads, axis=0)
    grad_features = (back * style[:, :, None]).astype(jnp.bfloat16)
    return (styled, grad_weight, grad_features)
```

```python
import jax
import jax.numpy as jnp
from jax import lax
from jax.experimental import pallas as pl
from jax.experimental.pallas import tpu as pltpu
from jax.sharding import PartitionSpec as P

WIDTH = 64
ROWS = 8


OFFSETS = [(-1, -1), (-1, 0), (-1, 1), (0, -1), (0, 0), (0, 1), (1, -1), (1, 0), (1, 1)]
EPSILON = 1e-08


def moved(array, row_step, col_step):
    count = array.shape[0]
    depth = array.shape[1]
    grid = array.reshape(count, depth, ROWS, WIDTH)
    padded = jnp.pad(grid, ((0, 0), (0, 0), (1, 1), (1, 1)))
    part = padded[:, :, 1 + row_step : 1 + row_step + ROWS, 1 + col_step : 1 + col_step + WIDTH]
    return part.reshape(count, depth, ROWS * WIDTH)


def per_device(features, weight, style, bias, adjoint):
    local_ch = features.shape[1]
    sect_count = lax.axis_size("sect")
    sect_place = lax.axis_index("sect")
    channels = local_ch * sect_count
    samples = features.shape[0]
    pixels = features.shape[2]
    own_style = lax.dynamic_slice_in_dim(style, sect_place * local_ch, local_ch, 1)
    local_mod = (features.astype(jnp.float32) * own_style[:, :, None]).astype(jnp.bfloat16)
    modulated = lax.all_gather(local_mod, "sect", axis=1, tiled=True)
    full_weight = lax.all_gather(weight, "sample", axis=0, tiled=True)
    kernel = full_weight.reshape(9, channels, local_ch)
    kernel_f = kernel.astype(jnp.float32)
    shifts = [moved(modulated, row_step, col_step) for row_step, col_step in OFFSETS]
    conv_out = jnp.zeros(features.shape, jnp.float32)
    for index in range(9):
        conv_out = conv_out + jnp.einsum(
            "nip,io->nop", shifts[index], kernel[index], preferred_element_type=jnp.float32
        )
    kernel_sq = jnp.sum(kernel_f * kernel_f, axis=0)
    style_sq = style * style
    energy = jnp.dot(style_sq, kernel_sq, precision=lax.Precision.HIGHEST) + EPSILON
    demod = lax.rsqrt(energy)
    styled = (conv_out * demod[:, :, None] + bias[None, :, None]).astype(jnp.bfloat16)
    adjoint_f = adjoint.astype(jnp.float32)
    scaled_adjoint = (adjoint_f * demod[:, :, None]).astype(jnp.bfloat16)
    demod_grad = jnp.sum(adjoint_f * conv_out, axis=2)
    energy_grad = -0.5 * demod_grad * demod * demod * demod
    coupling = jnp.dot(style_sq.T, energy_grad, precision=lax.Precision.HIGHEST)
    grads = []
    for index in range(9):
        grads.append(
            jnp.einsum(
                "nip,nop->io", shifts[index], scaled_adjoint, preferred_element_type=jnp.float32
            )
            + 2.0 * kernel_f[index] * coupling
        )
    grad_terms = jnp.concatenate(grads, axis=0)
    grad_weight = lax.psum_scatter(grad_terms, ("sample", "dom"), scatter_dimension=0, tiled=True)
    back = jnp.zeros((samples, channels, pixels), jnp.float32)
    for index in range(9):
        row_step, col_step = OFFSETS[index]
        partial_back = jnp.einsum(
            "nop,io->nip", scaled_adjoint, kernel[index], preferred_element_type=jnp.float32
        )
        back = back + moved(partial_back, -row_step, -col_step)
    summed = lax.psum_scatter(back, "sect", scatter_dimension=1, tiled=True)
    grad_features = (summed * own_style[:, :, None]).astype(jnp.bfloat16)
    return (styled, grad_weight, grad_features)


MESH = pl.DeviceIdType.MESH
HIGH = lax.Precision.HIGHEST
F32 = jnp.float32
BF16 = jnp.bfloat16
CH = 512
BLOCK = 128
PIXELS = ROWS * WIDTH
OWN = 1152
HALF = 576


def fits(mesh):
    return mesh.shape["sample"] == 4 and mesh.shape["sect"] == 4 and mesh.shape["dom"] == 2


def shifted_by(array, row_step, col_step):
    step = row_step * WIDTH + col_step
    if step == 0:
        return array
    place = lax.broadcasted_iota(jnp.int32, (1, PIXELS), 1)
    col = jnp.bitwise_and(place, WIDTH - 1) + col_step
    full = place + row_step * WIDTH
    ok = (col >= 0) & (col < WIDTH) & (full >= 0) & (full < PIXELS)
    rolled = pltpu.roll(array, (-step) % PIXELS, 1)
    return jnp.where(ok, rolled, 0.0)


def column(row):
    return jnp.transpose(jnp.broadcast_to(row, (BLOCK, BLOCK)))[:, 0:1]


def as_row(col):
    return jnp.transpose(jnp.broadcast_to(col, (BLOCK, BLOCK)))[0:1, :]


def fused_kernel(
    features, weight, style, bias, adjoint, styled, grad_weight, grad_features,
    kern, mod, adj, grad, grad_b, from_dom, to_sample, from_sample, to_sect, from_sect,
    twice, style_all, energy_out, energy_in, egrad_all,
    style_s, style_r, mod_s, mod_r, w_s, w_r, w2_s, w2_r, en_s, en_r,
    gy_s, gy_r, gz_s, gz_r, bk_s, bk_r, eg_s, eg_r, swap_s, swap_r,
):
    s = lax.axis_index("sample")
    c = lax.axis_index("sect")
    d = lax.axis_index("dom")
    other = 1 - d

    def at_sample(k):
        return {"sample": lax.rem(s + k, 4)}

    def at_sect(k):
        return {"sect": lax.rem(c + k, 4)}

    partner = {"dom": other}

    def remote(src, dst, send, recv, where):
        return pltpu.make_async_remote_copy(
            src_ref=src, dst_ref=dst, send_sem=send, recv_sem=recv, device_id=where, device_id_type=MESH
        )

    barrier = pltpu.get_barrier_semaphore()
    for k in (1, 2, 3):
        pl.semaphore_signal(barrier, inc=1, device_id=at_sample(k), device_id_type=MESH)
        pl.semaphore_signal(barrier, inc=1, device_id=at_sect(k), device_id_type=MESH)
    pl.semaphore_signal(barrier, inc=1, device_id=partner, device_id_type=MESH)

    own_channels = pl.ds(pl.multiple_of(c * BLOCK, BLOCK), BLOCK)
    style_col = column(style[:, own_channels])
    mod[own_channels, :] = (features[0].astype(F32) * style_col).astype(BF16)
    style_all[0, 0] = style[...]
    own_rows = pl.ds(pl.multiple_of(s * OWN, OWN), OWN)
    kern[own_rows, :] = weight[...]

    def rows_of(shard, part):
        return pl.ds(pl.multiple_of(shard * OWN + part * HALF, HALF), HALF)

    pl.semaphore_wait(barrier, 7)

    style_c = [
        remote(style_all.at[0, 0], style_all.at[0, k], style_s.at[k], style_r.at[k], at_sample(k)) for k in (1, 2, 3)
    ]
    for copy in style_c:
        copy.start()
    mod_c = [
        remote(mod.at[own_channels], mod.at[own_channels], mod_s.at[k], mod_r.at[k], at_sect(k)) for k in (1, 2, 3)
    ]
    for copy in mod_c:
        copy.start()
    w_c = [
        remote(
            weight.at[pl.ds(pl.multiple_of(d * HALF, HALF), HALF)],
            kern.at[rows_of(s, d)],
            w_s.at[k],
            w_r.at[k],
            at_sample(k),
        )
        for k in (1, 2, 3)
    ]
    for k in (2, 1, 3):
        w_c[k - 1].start()

    squares = weight[...].astype(F32)
    squares = squares * squares
    part = squares[0:CH] + squares[CH : 2 * CH]
    tail = part[0:BLOCK] + squares[2 * CH : OWN]
    twice[0:BLOCK] = tail
    twice[BLOCK:CH] = part[BLOCK:]
    twice[CH : CH + BLOCK] = tail
    twice[CH + BLOCK : 2 * CH] = part[BLOCK:]
    kernel_sq = twice[pl.ds(pl.multiple_of(CH - s * BLOCK, BLOCK), CH), :]
    for copy in style_c:
        copy.wait_recv()
    swap_style = remote(style_all.at[0], style_all.at[1], swap_s.at[0], swap_r.at[0], partner)
    swap_style.start()
    styles = jnp.concatenate([style_all[0, k] for k in range(4)] * 2, axis=0)
    terms = jnp.dot(styles * styles, kernel_sq, precision=HIGH, preferred_element_type=F32)
    for k in range(4):
        energy_out[k] = terms[k : k + 1, :]
    en_c = [
        remote(energy_out.at[k], energy_in.at[k], en_s.at[k], en_r.at[k], at_sample(4 - k)) for k in (1, 2, 3)
    ]
    for copy in en_c:
        copy.start()
    energy = energy_out[0] + EPSILON
    for k in (1, 2, 3):
        en_c[k - 1].wait_recv()
        energy = energy + energy_in[k]
    demod = column(lax.rsqrt(energy))

    adjoint_f = adjoint[0].astype(F32)
    scaled = (adjoint_f * demod).astype(BF16).astype(F32)
    for index in range(9):
        row_step, col_step = OFFSETS[index]
        adj[index * BLOCK : (index + 1) * BLOCK, :] = shifted_by(scaled, -row_step, -col_step).astype(BF16)
    for copy in mod_c:
        copy.wait_recv()

    for index in range(9):
        value = lax.dot_general(
            mod[...],
            adj[index * BLOCK : (index + 1) * BLOCK, :],
            (((1,), (1,)), ((), ())),
            preferred_element_type=F32,
        )
        grad[index * CH : (index + 1) * CH, :] = value
        grad_b[index * CH : (index + 1) * CH, :] = value.astype(BF16)
    gy_c = [
        remote(
            grad_b.at[rows_of(lax.rem(s + k, 4), other)], from_dom.at[k], gy_s.at[k], gy_r.at[k], partner
        )
        for k in range(4)
    ]
    order = (2, 1, 3, 0)
    for k in order:
        gy_c[k].start()

    w2_c = []
    for k in (1, 3, 2):
        shard = lax.rem(s + 4 - k, 4)
        w_c[k - 1].wait_recv()
        copy = remote(kern.at[rows_of(shard, d)], kern.at[rows_of(shard, d)], w2_s.at[k], w2_r.at[k], partner)
        copy.start()
        w2_c.append(copy)

    gz_c = []
    for k in (2, 1, 3):
        gy_c[k].wait_recv()
        kept = grad[rows_of(lax.rem(s + k, 4), d), :]
        to_sample[k] = (kept + from_dom[k].astype(F32)).astype(BF16)
        copy = remote(to_sample.at[k], from_sample.at[k], gz_s.at[k], gz_r.at[k], at_sample(k))
        copy.start()
        gz_c.append(copy)

    for copy in w2_c:
        copy.wait_recv()

    wide = adj[...]

    def back_of(block):
        rows = [
            kern[pl.ds(pl.multiple_of(index * CH + block * BLOCK, BLOCK), BLOCK), :] for index in range(9)
        ]
        return jnp.dot(jnp.concatenate(rows, axis=1), wide, preferred_element_type=F32)

    bk_c = []
    for k in (2, 1, 3):
        to_sect[k] = back_of(lax.rem(c + k, 4)).astype(BF16)
        copy = remote(to_sect.at[k], from_sect.at[k], bk_s.at[k], bk_r.at[k], at_sect(k))
        copy.start()
        bk_c.append(copy)

    conv_out = jnp.zeros((BLOCK, PIXELS), F32)
    for index in range(9):
        row_step, col_step = OFFSETS[index]
        value = lax.dot_general(
            kern[index * CH : (index + 1) * CH, :],
            mod[...],
            (((0,), (0,)), ((), ())),
            preferred_element_type=F32,
        )
        conv_out = conv_out + shifted_by(value, row_step, col_step)
    demod_grad = jnp.sum(adjoint_f * conv_out, axis=1, keepdims=True)
    egrad_all[0, 0] = as_row(-0.5 * demod_grad * demod * demod * demod)
    eg_c = [
        remote(egrad_all.at[0, 0], egrad_all.at[0, k], eg_s.at[k], eg_r.at[k], at_sample(k)) for k in (1, 2, 3)
    ]
    for copy in eg_c:
        copy.start()
    styled[0] = (conv_out * demod + column(bias[...])).astype(BF16)
    own_back = back_of(c)
    for copy in eg_c:
        copy.wait_recv()
    swap_egrad = remote(egrad_all.at[0], egrad_all.at[1], swap_s.at[1], swap_r.at[1], partner)
    swap_egrad.start()

    gy_c[0].wait_recv()
    total = grad[rows_of(s, d), :] + from_dom[0].astype(F32)
    for k, copy in zip((2, 1, 3), gz_c):
        copy.wait_recv()
        total = total + from_sample[k].astype(F32)

    swap_style.wait_recv()
    swap_egrad.wait_recv()
    styles = jnp.concatenate([style_all[h, k] for h in range(2) for k in range(4)], axis=0)
    egrads = jnp.concatenate([egrad_all[h, k] for h in range(2) for k in range(4)], axis=0)
    coupling = lax.dot_general(
        styles * styles, egrads, (((0,), (0,)), ((), ())), precision=HIGH, preferred_element_type=F32
    )
    twice[0:CH] = coupling
    twice[CH : 2 * CH] = coupling
    first = pl.multiple_of((2 * s + d) * (HALF - CH), HALF - CH)
    owned = weight[pl.ds(pl.multiple_of(d * HALF, HALF), HALF), :].astype(F32)
    grad_weight[...] = total + 2.0 * owned * twice[pl.ds(first, HALF), :]

    summed = own_back
    for k, copy in zip((2, 1, 3), bk_c):
        copy.wait_recv()
        summed = summed + from_sect[k].astype(F32)
    grad_features[0] = (summed * style_col).astype(BF16)

    for copy in style_c + mod_c + w_c + w2_c + en_c + gy_c + gz_c + bk_c + eg_c + [swap_style, swap_egrad]:
        copy.wait_send()


def fused(features, weight, style, bias, adjoint):
    vmem = pl.BlockSpec(memory_space=pltpu.VMEM)
    dma = pltpu.SemaphoreType.DMA((4,))
    return tuple(
        pl.pallas_call(
            fused_kernel,
            out_shape=(
                jax.ShapeDtypeStruct(features.shape, BF16),
                jax.ShapeDtypeStruct((HALF, BLOCK), F32),
                jax.ShapeDtypeStruct(features.shape, BF16),
            ),
            in_specs=[vmem] * 5,
            out_specs=(vmem,) * 3,
            scratch_shapes=[
                pltpu.VMEM((9 * CH, BLOCK), BF16),
                pltpu.VMEM((CH, PIXELS), BF16),
                pltpu.VMEM((9 * BLOCK, PIXELS), BF16),
                pltpu.VMEM((9 * CH, BLOCK), F32),
                pltpu.VMEM((9 * CH, BLOCK), BF16),
                pltpu.VMEM((4, HALF, BLOCK), BF16),
                pltpu.VMEM((4, HALF, BLOCK), BF16),
                pltpu.VMEM((4, HALF, BLOCK), BF16),
                pltpu.VMEM((4, BLOCK, PIXELS), BF16),
                pltpu.VMEM((4, BLOCK, PIXELS), BF16),
                pltpu.VMEM((2 * CH, BLOCK), F32),
                pltpu.VMEM((2, 4, 1, CH), F32),
                pltpu.VMEM((4, 1, BLOCK), F32),
                pltpu.VMEM((4, 1, BLOCK), F32),
                pltpu.VMEM((2, 4, 1, BLOCK), F32),
            ]
            + [dma] * 20,
            compiler_params=pltpu.CompilerParams(
                collective_id=0, has_side_effects=True, vmem_limit_bytes=40 * 1024 * 1024
            ),
        )(features, weight, style, bias.reshape(1, BLOCK), adjoint)
    )


def solution(mesh):
    in_specs = (
        P(("sample", "dom"), "sect", None),
        P("sample", "sect"),
        P(("sample", "dom"), None),
        P("sect"),
        P(("sample", "dom"), "sect", None),
    )
    out_specs = (
        P(("sample", "dom"), "sect", None),
        P(("sample", "dom"), "sect"),
        P(("sample", "dom"), "sect", None),
    )
    body = fused if fits(mesh) else per_device
    return jax.shard_map(
        body, mesh=mesh, in_specs=in_specs, out_specs=out_specs, check_vma=False
    )
```

```python
import jax
import jax.numpy as jnp
from jax import lax
from jax.experimental import pallas as pl
from jax.experimental.pallas import tpu as pltpu
from jax.sharding import PartitionSpec as P

WIDTH = 64
ROWS = 8


OFFSETS = [(-1, -1), (-1, 0), (-1, 1), (0, -1), (0, 0), (0, 1), (1, -1), (1, 0), (1, 1)]
EPSILON = 1e-08


def moved(array, row_step, col_step):
    count = array.shape[0]
    depth = array.shape[1]
    grid = array.reshape(count, depth, ROWS, WIDTH)
    padded = jnp.pad(grid, ((0, 0), (0, 0), (1, 1), (1, 1)))
    part = padded[:, :, 1 + row_step : 1 + row_step + ROWS, 1 + col_step : 1 + col_step + WIDTH]
    return part.reshape(count, depth, ROWS * WIDTH)


def per_device(features, weight, style, bias, adjoint):
    local_ch = features.shape[1]
    sect_count = lax.axis_size("sect")
    sect_place = lax.axis_index("sect")
    channels = local_ch * sect_count
    samples = features.shape[0]
    pixels = features.shape[2]
    own_style = lax.dynamic_slice_in_dim(style, sect_place * local_ch, local_ch, 1)
    local_mod = (features.astype(jnp.float32) * own_style[:, :, None]).astype(jnp.bfloat16)
    modulated = lax.all_gather(local_mod, "sect", axis=1, tiled=True)
    full_weight = lax.all_gather(weight, "sample", axis=0, tiled=True)
    kernel = full_weight.reshape(9, channels, local_ch)
    kernel_f = kernel.astype(jnp.float32)
    shifts = [moved(modulated, row_step, col_step) for row_step, col_step in OFFSETS]
    conv_out = jnp.zeros(features.shape, jnp.float32)
    for index in range(9):
        conv_out = conv_out + jnp.einsum(
            "nip,io->nop", shifts[index], kernel[index], preferred_element_type=jnp.float32
        )
    kernel_sq = jnp.sum(kernel_f * kernel_f, axis=0)
    style_sq = style * style
    energy = jnp.dot(style_sq, kernel_sq, precision=lax.Precision.HIGHEST) + EPSILON
    demod = lax.rsqrt(energy)
    styled = (conv_out * demod[:, :, None] + bias[None, :, None]).astype(jnp.bfloat16)
    adjoint_f = adjoint.astype(jnp.float32)
    scaled_adjoint = (adjoint_f * demod[:, :, None]).astype(jnp.bfloat16)
    demod_grad = jnp.sum(adjoint_f * conv_out, axis=2)
    energy_grad = -0.5 * demod_grad * demod * demod * demod
    coupling = jnp.dot(style_sq.T, energy_grad, precision=lax.Precision.HIGHEST)
    grads = []
    for index in range(9):
        grads.append(
            jnp.einsum(
                "nip,nop->io", shifts[index], scaled_adjoint, preferred_element_type=jnp.float32
            )
            + 2.0 * kernel_f[index] * coupling
        )
    grad_terms = jnp.concatenate(grads, axis=0)
    grad_weight = lax.psum_scatter(grad_terms, ("sample", "dom"), scatter_dimension=0, tiled=True)
    back = jnp.zeros((samples, channels, pixels), jnp.float32)
    for index in range(9):
        row_step, col_step = OFFSETS[index]
        partial_back = jnp.einsum(
            "nop,io->nip", scaled_adjoint, kernel[index], preferred_element_type=jnp.float32
        )
        back = back + moved(partial_back, -row_step, -col_step)
    summed = lax.psum_scatter(back, "sect", scatter_dimension=1, tiled=True)
    grad_features = (summed * own_style[:, :, None]).astype(jnp.bfloat16)
    return (styled, grad_weight, grad_features)


MESH = pl.DeviceIdType.MESH
HIGH = lax.Precision.HIGHEST
F32 = jnp.float32
BF16 = jnp.bfloat16
CH = 512
BLOCK = 128
PIXELS = ROWS * WIDTH
OWN = 1152
HALF = 576


def fits(mesh):
    return mesh.shape["sample"] == 4 and mesh.shape["sect"] == 4 and mesh.shape["dom"] == 2


def moved_rows(array, row_step, col_step):
    if col_step != 0:
        place = lax.broadcasted_iota(jnp.int32, (PIXELS, 1), 0)
        col = jnp.bitwise_and(place, WIDTH - 1) + col_step
        array = jnp.where((col >= 0) & (col < WIDTH), pltpu.roll(array, (-col_step) % PIXELS, 0), 0.0)
    edge = jnp.zeros((WIDTH, array.shape[1]), array.dtype)
    if row_step == 1:
        array = jnp.concatenate([array[WIDTH:], edge], axis=0)
    if row_step == -1:
        array = jnp.concatenate([edge, array[:-WIDTH]], axis=0)
    return array


def column(row):
    return jnp.transpose(jnp.broadcast_to(row, (BLOCK, BLOCK)))[:, 0:1]


def as_row(col):
    return jnp.transpose(jnp.broadcast_to(col, (BLOCK, BLOCK)))[0:1, :]


def fused_kernel(
    features_h, weight_h, style_h, bias_h, adjoint_h, styled, grad_weight, grad_features,
    features, bias, adjoint, in_s, kern, mod, mod_t, adj, grad, grad_b, from_dom, to_sample, from_sample, to_sect, from_sect,
    twice, style_all, energy_out, energy_in, egrad_all,
    style_s, style_r, mod_s, mod_r, w_s, w_r, w2_s, w2_r, en_s, en_r,
    gy_s, gy_r, gz_s, gz_r, bk_s, bk_r, eg_s, eg_r, swap_s, swap_r,
):
    s = lax.axis_index("sample")
    c = lax.axis_index("sect")
    d = lax.axis_index("dom")
    other = 1 - d

    def at_sample(k):
        return {"sample": lax.rem(s + k, 4)}

    def at_sect(k):
        return {"sect": lax.rem(c + k, 4)}

    partner = {"dom": other}

    def remote(src, dst, send, recv, where):
        return pltpu.make_async_remote_copy(
            src_ref=src, dst_ref=dst, send_sem=send, recv_sem=recv, device_id=where, device_id_type=MESH
        )

    style_all_own = style_all.at[0, 0]
    own_rows = pl.ds(pl.multiple_of(s * OWN, OWN), OWN)
    loads = [
        pltpu.make_async_copy(source, target, in_s.at[index])
        for index, (source, target) in enumerate(
            (
                (style_h, style_all_own),
                (features_h.at[0], features),
                (weight_h, kern.at[own_rows]),
                (adjoint_h.at[0], adjoint),
                (bias_h, bias),
            )
        )
    ]
    for load in loads:
        load.start()

    barrier = pltpu.get_barrier_semaphore()
    for k in (1, 2, 3):
        pl.semaphore_signal(barrier, inc=1, device_id=at_sample(k), device_id_type=MESH)
        pl.semaphore_signal(barrier, inc=1, device_id=at_sect(k), device_id_type=MESH)
    pl.semaphore_signal(barrier, inc=1, device_id=partner, device_id_type=MESH)

    own_channels = pl.ds(pl.multiple_of(c * BLOCK, BLOCK), BLOCK)
    for load in loads[0:3]:
        load.wait()
    style_col = column(style_all[0, 0, :, own_channels])
    mod[own_channels, :] = (features[...].astype(F32) * style_col).astype(BF16)

    def rows_of(shard, part):
        return pl.ds(pl.multiple_of(shard * OWN + part * HALF, HALF), HALF)

    def along(up, j):
        half = kern.at[rows_of(s - j if up else s + j, d)]
        slot = j if up else 3 + j
        return remote(half, half, w_s.at[slot], w_r.at[slot], at_sample(1 if up else 3))

    def across(up, j):
        half = kern.at[rows_of(s - 1 - j if up else s + 1 + j, d)]
        slot = j if up else 3 + j
        return remote(half, half, w2_s.at[slot], w2_r.at[slot], partner)

    def sends(up, j):
        return (s >= j) & (s < 3) if up else (s <= 3 - j) & (s > 0)

    def gets(up, j):
        return s >= j + 1 if up else s <= 2 - j

    def pass_on(j):
        for up in (True, False):

            @pl.when(gets(up, j))
            def _():
                along(up, j).wait_recv()
                across(up, j).start()

            if j < 2:

                @pl.when(sends(up, j + 1))
                def _():
                    along(up, j + 1).start()

    squares = kern[own_rows, :].astype(F32)
    squares = squares * squares
    part = squares[0:CH] + squares[CH : 2 * CH]
    tail = part[0:BLOCK] + squares[2 * CH : OWN]
    twice[0:BLOCK] = tail
    twice[BLOCK:CH] = part[BLOCK:]
    twice[CH : CH + BLOCK] = tail
    twice[CH + BLOCK : 2 * CH] = part[BLOCK:]
    kernel_sq = twice[pl.ds(pl.multiple_of(CH - s * BLOCK, BLOCK), CH), :]

    pl.semaphore_wait(barrier, 7)

    style_c = [
        remote(style_all.at[0, 0], style_all.at[0, k], style_s.at[k], style_r.at[k], at_sample(k)) for k in (1, 2, 3)
    ]
    for copy in style_c:
        copy.start()
    for up in (True, False):

        @pl.when(sends(up, 0))
        def _():
            along(up, 0).start()

    mod_c = [
        remote(mod.at[own_channels], mod.at[own_channels], mod_s.at[k], mod_r.at[k], at_sect(k)) for k in (1, 2, 3)
    ]
    for copy in mod_c:
        copy.start()
    for copy in style_c:
        copy.wait_recv()
    swap_style = remote(style_all.at[0], style_all.at[1], swap_s.at[0], swap_r.at[0], partner)
    swap_style.start()
    styles = jnp.concatenate([style_all[0, k] for k in range(4)] * 2, axis=0)
    terms = jnp.dot(styles * styles, kernel_sq, precision=HIGH, preferred_element_type=F32)
    for k in range(4):
        energy_out[k] = terms[k : k + 1, :]
    en_c = [
        remote(energy_out.at[k], energy_in.at[k], en_s.at[k], en_r.at[k], at_sample(4 - k)) for k in (1, 2, 3)
    ]
    for copy in en_c:
        copy.start()
    pass_on(0)
    energy = energy_out[0] + EPSILON
    for k in (1, 2, 3):
        en_c[k - 1].wait_recv()
        energy = energy + energy_in[k]
    demod = column(lax.rsqrt(energy))

    loads[3].wait()
    loads[4].wait()
    adjoint_f = adjoint[...].astype(F32)
    scaled = (adjoint_f * demod).astype(BF16).astype(F32)
    scaled_t = jnp.transpose(scaled)
    for col_step in (-1, 0, 1):
        by_col = moved_rows(scaled_t, 0, -col_step)
        for row_step in (-1, 0, 1):
            index = OFFSETS.index((row_step, col_step))
            adj[:, index * BLOCK : (index + 1) * BLOCK] = moved_rows(by_col, -row_step, 0).astype(BF16)
    for copy in mod_c:
        copy.wait_recv()
    pass_on(1)

    for index in range(0, 9, 2):
        last = min(index + 2, 9)
        value = jnp.dot(mod[...], adj[:, index * BLOCK : last * BLOCK], preferred_element_type=F32)
        for one in range(index, last):
            block = value[:, (one - index) * BLOCK : (one - index + 1) * BLOCK]
            grad[one * CH : (one + 1) * CH, :] = block
            grad_b[one * CH : (one + 1) * CH, :] = block.astype(BF16)
    gy_c = [
        remote(
            grad_b.at[rows_of(lax.rem(s + k, 4), other)], from_dom.at[k], gy_s.at[k], gy_r.at[k], partner
        )
        for k in range(4)
    ]
    order = (2, 1, 3, 0)
    for k in order:
        gy_c[k].start()

    pass_on(2)
    mod_t[...] = jnp.transpose(mod[...])
    for j in range(3):
        for up in (True, False):

            @pl.when(gets(up, j))
            def _():
                across(up, j).wait_recv()

    wide = adj[...]

    def back_of(block):
        rows = [
            kern[pl.ds(pl.multiple_of(index * CH + block * BLOCK, BLOCK), BLOCK), :] for index in range(9)
        ]
        return lax.dot_general(
            jnp.concatenate(rows, axis=1), wide, (((1,), (1,)), ((), ())), preferred_element_type=F32
        )

    bk_c = []
    for k in (2, 1, 3):
        to_sect[k] = back_of(lax.rem(c + k, 4)).astype(BF16)
        copy = remote(to_sect.at[k], from_sect.at[k], bk_s.at[k], bk_r.at[k], at_sect(k))
        copy.start()
        bk_c.append(copy)

    conv_t = jnp.zeros((PIXELS, BLOCK), F32)
    for col_step in (-1, 0, 1):
        three = [OFFSETS.index((row_step, col_step)) * CH for row_step in (-1, 0, 1)]
        value = jnp.dot(
            mod_t[...],
            jnp.concatenate([kern[row : row + CH, :] for row in three], axis=1),
            preferred_element_type=F32,
        )
        by_row = value[:, BLOCK : 2 * BLOCK]
        by_row = by_row + moved_rows(value[:, 0:BLOCK], -1, 0) + moved_rows(value[:, 2 * BLOCK :], 1, 0)
        conv_t = conv_t + moved_rows(by_row, 0, col_step)
    conv_out = jnp.transpose(conv_t)
    demod_grad = jnp.sum(adjoint_f * conv_out, axis=1, keepdims=True)
    egrad_all[0, 0] = as_row(-0.5 * demod_grad * demod * demod * demod)
    eg_c = [
        remote(egrad_all.at[0, 0], egrad_all.at[0, k], eg_s.at[k], eg_r.at[k], at_sample(k)) for k in (1, 2, 3)
    ]
    for copy in eg_c:
        copy.start()
    styled[0] = (conv_out * demod + column(bias[...])).astype(BF16)
    gz_c = []
    for k in (2, 1, 3):
        gy_c[k].wait_recv()
        kept = grad[rows_of(lax.rem(s + k, 4), d), :]
        to_sample[k] = (kept + from_dom[k].astype(F32)).astype(BF16)
        copy = remote(to_sample.at[k], from_sample.at[k], gz_s.at[k], gz_r.at[k], at_sample(k))
        copy.start()
        gz_c.append(copy)

    own_back = back_of(c)
    for copy in eg_c:
        copy.wait_recv()
    swap_egrad = remote(egrad_all.at[0], egrad_all.at[1], swap_s.at[1], swap_r.at[1], partner)
    swap_egrad.start()

    gy_c[0].wait_recv()
    total = grad[rows_of(s, d), :] + from_dom[0].astype(F32)
    for k, copy in zip((2, 1, 3), gz_c):
        copy.wait_recv()
        total = total + from_sample[k].astype(F32)

    swap_style.wait_recv()
    swap_egrad.wait_recv()
    styles = jnp.concatenate([style_all[h, k] for h in range(2) for k in range(4)], axis=0)
    egrads = jnp.concatenate([egrad_all[h, k] for h in range(2) for k in range(4)], axis=0)
    coupling = lax.dot_general(
        styles * styles, egrads, (((0,), (0,)), ((), ())), precision=HIGH, preferred_element_type=F32
    )
    twice[0:CH] = coupling
    twice[CH : 2 * CH] = coupling
    first = pl.multiple_of((2 * s + d) * (HALF - CH), HALF - CH)
    owned = kern[rows_of(s, d), :].astype(F32)
    grad_weight[...] = total + 2.0 * owned * twice[pl.ds(first, HALF), :]

    summed = own_back
    for k, copy in zip((2, 1, 3), bk_c):
        copy.wait_recv()
        summed = summed + from_sect[k].astype(F32)
    grad_features[0] = (summed * style_col).astype(BF16)

    for copy in style_c + mod_c + en_c + gy_c + gz_c + bk_c + eg_c + [swap_style, swap_egrad]:
        copy.wait_send()
    for j in range(3):
        for up in (True, False):

            @pl.when(sends(up, j))
            def _():
                along(up, j).wait_send()

            @pl.when(gets(up, j))
            def _():
                across(up, j).wait_send()


def fused(features, weight, style, bias, adjoint):
    vmem = pl.BlockSpec(memory_space=pltpu.VMEM)
    dma = pltpu.SemaphoreType.DMA((6,))
    return tuple(
        pl.pallas_call(
            fused_kernel,
            out_shape=(
                jax.ShapeDtypeStruct(features.shape, BF16),
                jax.ShapeDtypeStruct((HALF, BLOCK), F32),
                jax.ShapeDtypeStruct(features.shape, BF16),
            ),
            in_specs=[pl.BlockSpec(memory_space=pltpu.HBM)] * 5,
            out_specs=(vmem,) * 3,
            scratch_shapes=[
                pltpu.VMEM((BLOCK, PIXELS), BF16),
                pltpu.VMEM((1, BLOCK), F32),
                pltpu.VMEM((BLOCK, PIXELS), BF16),
                pltpu.SemaphoreType.DMA((5,)),
                pltpu.VMEM((9 * CH, BLOCK), BF16),
                pltpu.VMEM((CH, PIXELS), BF16),
                pltpu.VMEM((PIXELS, CH), BF16),
                pltpu.VMEM((PIXELS, 9 * BLOCK), BF16),
                pltpu.VMEM((9 * CH, BLOCK), F32),
                pltpu.VMEM((9 * CH, BLOCK), BF16),
                pltpu.VMEM((4, HALF, BLOCK), BF16),
                pltpu.VMEM((4, HALF, BLOCK), BF16),
                pltpu.VMEM((4, HALF, BLOCK), BF16),
                pltpu.VMEM((4, BLOCK, PIXELS), BF16),
                pltpu.VMEM((4, BLOCK, PIXELS), BF16),
                pltpu.VMEM((2 * CH, BLOCK), F32),
                pltpu.VMEM((2, 4, 1, CH), F32),
                pltpu.VMEM((4, 1, BLOCK), F32),
                pltpu.VMEM((4, 1, BLOCK), F32),
                pltpu.VMEM((2, 4, 1, BLOCK), F32),
            ]
            + [dma] * 20,
            compiler_params=pltpu.CompilerParams(
                collective_id=0, has_side_effects=True, vmem_limit_bytes=64 * 1024 * 1024
            ),
        )(features, weight, style, bias.reshape(1, BLOCK), adjoint)
    )


def solution(mesh):
    in_specs = (
        P(("sample", "dom"), "sect", None),
        P("sample", "sect"),
        P(("sample", "dom"), None),
        P("sect"),
        P(("sample", "dom"), "sect", None),
    )
    out_specs = (
        P(("sample", "dom"), "sect", None),
        P(("sample", "dom"), "sect"),
        P(("sample", "dom"), "sect", None),
    )
    body = fused if fits(mesh) else per_device
    return jax.shard_map(
        body, mesh=mesh, in_specs=in_specs, out_specs=out_specs, check_vma=False
    )
```

```python
import jax
import jax.numpy as jnp
from jax import lax
from jax.experimental import pallas as pl
from jax.experimental.pallas import tpu as pltpu
from jax.sharding import PartitionSpec as P

WIDTH = 64
ROWS = 8


OFFSETS = [(-1, -1), (-1, 0), (-1, 1), (0, -1), (0, 0), (0, 1), (1, -1), (1, 0), (1, 1)]
EPSILON = 1e-08


def moved(array, row_step, col_step):
    count = array.shape[0]
    depth = array.shape[1]
    grid = array.reshape(count, depth, ROWS, WIDTH)
    padded = jnp.pad(grid, ((0, 0), (0, 0), (1, 1), (1, 1)))
    part = padded[:, :, 1 + row_step : 1 + row_step + ROWS, 1 + col_step : 1 + col_step + WIDTH]
    return part.reshape(count, depth, ROWS * WIDTH)


def per_device(features, weight, style, bias, adjoint):
    local_ch = features.shape[1]
    sect_count = lax.axis_size("sect")
    sect_place = lax.axis_index("sect")
    channels = local_ch * sect_count
    samples = features.shape[0]
    pixels = features.shape[2]
    own_style = lax.dynamic_slice_in_dim(style, sect_place * local_ch, local_ch, 1)
    local_mod = (features.astype(jnp.float32) * own_style[:, :, None]).astype(jnp.bfloat16)
    modulated = lax.all_gather(local_mod, "sect", axis=1, tiled=True)
    full_weight = lax.all_gather(weight, "sample", axis=0, tiled=True)
    kernel = full_weight.reshape(9, channels, local_ch)
    kernel_f = kernel.astype(jnp.float32)
    shifts = [moved(modulated, row_step, col_step) for row_step, col_step in OFFSETS]
    conv_out = jnp.zeros(features.shape, jnp.float32)
    for index in range(9):
        conv_out = conv_out + jnp.einsum(
            "nip,io->nop", shifts[index], kernel[index], preferred_element_type=jnp.float32
        )
    kernel_sq = jnp.sum(kernel_f * kernel_f, axis=0)
    style_sq = style * style
    energy = jnp.dot(style_sq, kernel_sq, precision=lax.Precision.HIGHEST) + EPSILON
    demod = lax.rsqrt(energy)
    styled = (conv_out * demod[:, :, None] + bias[None, :, None]).astype(jnp.bfloat16)
    adjoint_f = adjoint.astype(jnp.float32)
    scaled_adjoint = (adjoint_f * demod[:, :, None]).astype(jnp.bfloat16)
    demod_grad = jnp.sum(adjoint_f * conv_out, axis=2)
    energy_grad = -0.5 * demod_grad * demod * demod * demod
    coupling = jnp.dot(style_sq.T, energy_grad, precision=lax.Precision.HIGHEST)
    grads = []
    for index in range(9):
        grads.append(
            jnp.einsum(
                "nip,nop->io", shifts[index], scaled_adjoint, preferred_element_type=jnp.float32
            )
            + 2.0 * kernel_f[index] * coupling
        )
    grad_terms = jnp.concatenate(grads, axis=0)
    grad_weight = lax.psum_scatter(grad_terms, ("sample", "dom"), scatter_dimension=0, tiled=True)
    back = jnp.zeros((samples, channels, pixels), jnp.float32)
    for index in range(9):
        row_step, col_step = OFFSETS[index]
        partial_back = jnp.einsum(
            "nop,io->nip", scaled_adjoint, kernel[index], preferred_element_type=jnp.float32
        )
        back = back + moved(partial_back, -row_step, -col_step)
    summed = lax.psum_scatter(back, "sect", scatter_dimension=1, tiled=True)
    grad_features = (summed * own_style[:, :, None]).astype(jnp.bfloat16)
    return (styled, grad_weight, grad_features)


MESH = pl.DeviceIdType.MESH
HIGH = lax.Precision.HIGHEST
F32 = jnp.float32
BF16 = jnp.bfloat16
CH = 512
BLOCK = 128
PIXELS = ROWS * WIDTH
OWN = 1152
HALF = 576


def fits(mesh):
    return mesh.shape["sample"] == 4 and mesh.shape["sect"] == 4 and mesh.shape["dom"] == 2


def moved_rows(array, row_step, col_step):
    if col_step != 0:
        place = lax.broadcasted_iota(jnp.int32, (PIXELS, 1), 0)
        col = jnp.bitwise_and(place, WIDTH - 1) + col_step
        array = jnp.where((col >= 0) & (col < WIDTH), pltpu.roll(array, (-col_step) % PIXELS, 0), 0.0)
    edge = jnp.zeros((WIDTH, array.shape[1]), array.dtype)
    if row_step == 1:
        array = jnp.concatenate([array[WIDTH:], edge], axis=0)
    if row_step == -1:
        array = jnp.concatenate([edge, array[:-WIDTH]], axis=0)
    return array


def column(row):
    return jnp.transpose(jnp.broadcast_to(row, (BLOCK, BLOCK)))[:, 0:1]


def fused_kernel(
    features_h, weight_h, style_h, bias_h, adjoint_h, styled, grad_weight, grad_features,
    features, bias, adjoint, in_s, kern, mod, mod_t, adj, adj_t, grad, given, from_dom, to_sample, from_sample, to_sect, from_sect,
    twice, style_all, energy_out, energy_in, egrad_all,
    style_s, style_r, mod_s, mod_r, w_s, w_r, w2_s, w2_r, en_s, en_r,
    gy_s, gy_r, gz_s, gz_r, bk_s, bk_r, eg_s, eg_r,
):
    s = lax.axis_index("sample")
    c = lax.axis_index("sect")
    d = lax.axis_index("dom")
    other = 1 - d

    def at_sample(k):
        return {"sample": lax.rem(s + k, 4)}

    def at_sect(k):
        return {"sect": lax.rem(c + k, 4)}

    def at_cross(k):
        return {"sample": lax.rem(s + k, 4), "dom": other}

    partner = {"dom": other}

    def remote(src, dst, send, recv, where):
        return pltpu.make_async_remote_copy(
            src_ref=src, dst_ref=dst, send_sem=send, recv_sem=recv, device_id=where, device_id_type=MESH
        )

    style_all_own = style_all.at[0, 0]
    own_rows = pl.ds(pl.multiple_of(s * OWN, OWN), OWN)
    loads = [
        pltpu.make_async_copy(source, target, in_s.at[index])
        for index, (source, target) in enumerate(
            (
                (style_h, style_all_own),
                (features_h.at[0], features),
                (weight_h, kern.at[own_rows]),
                (adjoint_h.at[0], adjoint),
                (bias_h, bias),
            )
        )
    ]
    for load in loads:
        load.start()

    barrier = pltpu.get_barrier_semaphore()
    for k in (1, 2, 3):
        for where in (at_sample(k), at_cross(k), at_sect(k)):
            pl.semaphore_signal(barrier, inc=1, device_id=where, device_id_type=MESH)
    pl.semaphore_signal(barrier, inc=1, device_id=partner, device_id_type=MESH)

    own_channels = pl.ds(pl.multiple_of(c * BLOCK, BLOCK), BLOCK)
    def rows_of(shard, part):
        return pl.ds(pl.multiple_of(shard * OWN + part * HALF, HALF), HALF)

    def along(up, j):
        half = kern.at[rows_of(s - j if up else s + j, d)]
        slot = j if up else 3 + j
        return remote(half, half, w_s.at[slot], w_r.at[slot], at_sample(1 if up else 3))

    def across(up, j):
        half = kern.at[rows_of(s - 1 - j if up else s + 1 + j, d)]
        slot = j if up else 3 + j
        return remote(half, half, w2_s.at[slot], w2_r.at[slot], partner)

    def sends(up, j):
        return (s >= j) & (s < 3) if up else (s <= 3 - j) & (s > 0)

    def gets(up, j):
        return s >= j + 1 if up else s <= 2 - j

    def pass_on(j):
        for up in (True, False):

            @pl.when(gets(up, j))
            def _():
                along(up, j).wait_recv()
                across(up, j).start()

            if j < 2:

                @pl.when(sends(up, j + 1))
                def _():
                    along(up, j + 1).start()

    def to_others(array, send, recv):
        peers = [(0, k, at_sample(k)) for k in (1, 2, 3)] + [(1, k, at_cross(k)) for k in range(4)]
        copies = [
            remote(array.at[0, 0], array.at[h, k], send.at[h, k], recv.at[h, k], where) for h, k, where in peers
        ]
        for copy in copies:
            copy.start()
        return copies

    loads[0].wait()
    loads[2].wait()
    pl.semaphore_wait(barrier, 10)

    style_c = to_others(style_all, style_s, style_r)
    for up in (True, False):

        @pl.when(sends(up, 0))
        def _():
            along(up, 0).start()

    loads[1].wait()
    style_col = column(style_all[0, 0, :, own_channels])
    mod[own_channels, :] = (features[...].astype(F32) * style_col).astype(BF16)

    mod_c = [
        remote(mod.at[own_channels], mod.at[own_channels], mod_s.at[k], mod_r.at[k], at_sect(k)) for k in (1, 2, 3)
    ]
    for copy in mod_c:
        copy.start()
    squares = kern[own_rows, :].astype(F32)
    squares = squares * squares
    part = squares[0:CH] + squares[CH : 2 * CH]
    tail = part[0:BLOCK] + squares[2 * CH : OWN]
    twice[0:BLOCK] = tail
    twice[BLOCK:CH] = part[BLOCK:]
    twice[CH : CH + BLOCK] = tail
    twice[CH + BLOCK : 2 * CH] = part[BLOCK:]
    kernel_sq = twice[pl.ds(pl.multiple_of(CH - s * BLOCK, BLOCK), CH), :]

    for copy in style_c[0:3]:
        copy.wait_recv()
    styles = jnp.concatenate([style_all[0, k] for k in range(4)] * 2, axis=0)
    terms = jnp.dot(styles * styles, kernel_sq, precision=HIGH, preferred_element_type=F32)
    for k in range(4):
        energy_out[k] = terms[k : k + 1, :]
    en_c = [
        remote(energy_out.at[k], energy_in.at[k], en_s.at[k], en_r.at[k], at_sample(4 - k)) for k in (1, 2, 3)
    ]
    for copy in en_c:
        copy.start()
    pass_on(0)

    loads[3].wait()
    loads[4].wait()
    adj_t[...] = jnp.transpose(adjoint[...].astype(F32))
    for col_step in (-1, 0, 1):
        by_col = moved_rows(adj_t[...], 0, -col_step)
        for row_step in (-1, 0, 1):
            index = OFFSETS.index((row_step, col_step))
            adj[:, index * BLOCK : (index + 1) * BLOCK] = moved_rows(by_col, -row_step, 0).astype(BF16)
    for copy in mod_c:
        copy.wait_recv()
    pass_on(1)

    for index in range(0, 9, 2):
        last = min(index + 2, 9)
        value = jnp.dot(mod[...], adj[:, index * BLOCK : last * BLOCK], preferred_element_type=F32)
        for one in range(index, last):
            grad[one * CH : (one + 1) * CH, :] = value[:, (one - index) * BLOCK : (one - index + 1) * BLOCK]
    energy = energy_out[0] + EPSILON
    for k in (1, 2, 3):
        en_c[k - 1].wait_recv()
        energy = energy + energy_in[k]
    demod = lax.rsqrt(energy)

    def kept(k):
        return grad[rows_of(lax.rem(s + k, 4), d), :] * demod

    def give(k):
        given[k] = (grad[rows_of(lax.rem(s + k, 4), other), :] * demod).astype(BF16)
        copy = remote(given.at[k], from_dom.at[k], gy_s.at[k], gy_r.at[k], partner)
        copy.start()
        return copy

    def hand_on(k):
        gy_c[k].wait_recv()
        to_sample[k] = (kept(k) + from_dom[k].astype(F32)).astype(BF16)
        copy = remote(to_sample.at[k], from_sample.at[k], gz_s.at[k], gz_r.at[k], at_sample(k))
        copy.start()
        return copy

    gy_c = {2: give(2), 1: give(1)}
    pass_on(2)
    gy_c[3] = give(3)
    gy_c[0] = give(0)
    mod_t[...] = jnp.transpose(mod[...])
    for index in range(9):
        part = slice(index * BLOCK, (index + 1) * BLOCK)
        adj[:, part] = (adj[:, part].astype(F32) * demod).astype(BF16)
    gz_c = [hand_on(2), hand_on(1)]
    for j in range(3):
        for up in (True, False):

            @pl.when(gets(up, j))
            def _():
                across(up, j).wait_recv()

    wide = adj[...]

    def back_of(block):
        rows = [
            kern[pl.ds(pl.multiple_of(index * CH + block * BLOCK, BLOCK), BLOCK), :] for index in range(9)
        ]
        return lax.dot_general(
            jnp.concatenate(rows, axis=1), wide, (((1,), (1,)), ((), ())), preferred_element_type=F32
        )

    bk_c = []
    for k in (2, 1, 3):
        to_sect[k] = back_of(lax.rem(c + k, 4)).astype(BF16)
        copy = remote(to_sect.at[k], from_sect.at[k], bk_s.at[k], bk_r.at[k], at_sect(k))
        copy.start()
        bk_c.append(copy)

    gz_c.append(hand_on(3))
    conv_t = jnp.zeros((PIXELS, BLOCK), F32)
    for col_step in (-1, 0, 1):
        three = [OFFSETS.index((row_step, col_step)) * CH for row_step in (-1, 0, 1)]
        value = jnp.dot(
            mod_t[...],
            jnp.concatenate([kern[row : row + CH, :] for row in three], axis=1),
            preferred_element_type=F32,
        )
        by_row = value[:, BLOCK : 2 * BLOCK]
        by_row = by_row + moved_rows(value[:, 0:BLOCK], -1, 0) + moved_rows(value[:, 2 * BLOCK :], 1, 0)
        conv_t = conv_t + moved_rows(by_row, 0, col_step)
    demod_grad = jnp.sum(adj_t[...] * conv_t, axis=0, keepdims=True)
    egrad_all[0, 0] = -0.5 * demod_grad * demod * demod * demod
    eg_c = to_others(egrad_all, eg_s, eg_r)
    styled[0] = jnp.transpose(conv_t * demod + bias[...]).astype(BF16)
    own_back = back_of(c)
    gy_c[0].wait_recv()
    total = kept(0) + from_dom[0].astype(F32)
    for k, copy in zip((2, 1, 3), gz_c):
        copy.wait_recv()
        total = total + from_sample[k].astype(F32)

    for copy in style_c[3:] + eg_c:
        copy.wait_recv()
    styles = jnp.concatenate([style_all[h, k] for h in range(2) for k in range(4)], axis=0)
    egrads = jnp.concatenate([egrad_all[h, k] for h in range(2) for k in range(4)], axis=0)
    coupling = lax.dot_general(
        styles * styles, egrads, (((0,), (0,)), ((), ())), precision=HIGH, preferred_element_type=F32
    )
    twice[0:CH] = coupling
    twice[CH : 2 * CH] = coupling
    first = pl.multiple_of((2 * s + d) * (HALF - CH), HALF - CH)
    owned = kern[rows_of(s, d), :].astype(F32)
    grad_weight[...] = total + 2.0 * owned * twice[pl.ds(first, HALF), :]

    summed = own_back
    for k, copy in zip((2, 1, 3), bk_c):
        copy.wait_recv()
        summed = summed + from_sect[k].astype(F32)
    grad_features[0] = (summed * style_col).astype(BF16)

    for copy in style_c + mod_c + en_c + list(gy_c.values()) + gz_c + bk_c + eg_c:
        copy.wait_send()
    for j in range(3):
        for up in (True, False):

            @pl.when(sends(up, j))
            def _():
                along(up, j).wait_send()

            @pl.when(gets(up, j))
            def _():
                across(up, j).wait_send()


def fused(features, weight, style, bias, adjoint):
    vmem = pl.BlockSpec(memory_space=pltpu.VMEM)
    dma = pltpu.SemaphoreType.DMA((6,))
    by_dom = pltpu.SemaphoreType.DMA((2, 4))
    return tuple(
        pl.pallas_call(
            fused_kernel,
            out_shape=(
                pltpu.VMEM(features.shape, BF16),
                pltpu.VMEM((HALF, BLOCK), F32),
                pltpu.VMEM(features.shape, BF16),
            ),
            in_specs=[pl.BlockSpec(memory_space=pltpu.HBM)] * 5,
            out_specs=(vmem,) * 3,
            scratch_shapes=[
                pltpu.VMEM((BLOCK, PIXELS), BF16),
                pltpu.VMEM((1, BLOCK), F32),
                pltpu.VMEM((BLOCK, PIXELS), BF16),
                pltpu.SemaphoreType.DMA((5,)),
                pltpu.VMEM((9 * CH, BLOCK), BF16),
                pltpu.VMEM((CH, PIXELS), BF16),
                pltpu.VMEM((PIXELS, CH), BF16),
                pltpu.VMEM((PIXELS, 9 * BLOCK), BF16),
                pltpu.VMEM((PIXELS, BLOCK), F32),
                pltpu.VMEM((9 * CH, BLOCK), F32),
                pltpu.VMEM((4, HALF, BLOCK), BF16),
                pltpu.VMEM((4, HALF, BLOCK), BF16),
                pltpu.VMEM((4, HALF, BLOCK), BF16),
                pltpu.VMEM((4, HALF, BLOCK), BF16),
                pltpu.VMEM((4, BLOCK, PIXELS), BF16),
                pltpu.VMEM((4, BLOCK, PIXELS), BF16),
                pltpu.VMEM((2 * CH, BLOCK), F32),
                pltpu.VMEM((2, 4, 1, CH), F32),
                pltpu.VMEM((4, 1, BLOCK), F32),
                pltpu.VMEM((4, 1, BLOCK), F32),
                pltpu.VMEM((2, 4, 1, BLOCK), F32),
            ]
            + [by_dom] * 2 + [dma] * 14 + [by_dom] * 2,
            compiler_params=pltpu.CompilerParams(
                collective_id=0, has_side_effects=True, vmem_limit_bytes=66478080
            ),
        )(features, weight, style, bias.reshape(1, BLOCK), adjoint)
    )


def solution(mesh):
    in_specs = (
        P(("sample", "dom"), "sect", None),
        P("sample", "sect"),
        P(("sample", "dom"), None),
        P("sect"),
        P(("sample", "dom"), "sect", None),
    )
    out_specs = (
        P(("sample", "dom"), "sect", None),
        P(("sample", "dom"), "sect"),
        P(("sample", "dom"), "sect", None),
    )
    body = fused if fits(mesh) else per_device
    return jax.shard_map(
        body, mesh=mesh, in_specs=in_specs, out_specs=out_specs, check_vma=False
    )
```

```python
import jax
import jax.numpy as jnp
from jax import lax
from jax.experimental import pallas as pl
from jax.experimental.pallas import tpu as pltpu
from jax.sharding import PartitionSpec as P

WIDTH = 64
ROWS = 8


OFFSETS = [(-1, -1), (-1, 0), (-1, 1), (0, -1), (0, 0), (0, 1), (1, -1), (1, 0), (1, 1)]
EPSILON = 1e-08


def moved(array, row_step, col_step):
    count = array.shape[0]
    depth = array.shape[1]
    grid = array.reshape(count, depth, ROWS, WIDTH)
    padded = jnp.pad(grid, ((0, 0), (0, 0), (1, 1), (1, 1)))
    part = padded[:, :, 1 + row_step : 1 + row_step + ROWS, 1 + col_step : 1 + col_step + WIDTH]
    return part.reshape(count, depth, ROWS * WIDTH)


def per_device(features, weight, style, bias, adjoint):
    local_ch = features.shape[1]
    sect_count = lax.axis_size("sect")
    sect_place = lax.axis_index("sect")
    channels = local_ch * sect_count
    samples = features.shape[0]
    pixels = features.shape[2]
    own_style = lax.dynamic_slice_in_dim(style, sect_place * local_ch, local_ch, 1)
    local_mod = (features.astype(jnp.float32) * own_style[:, :, None]).astype(jnp.bfloat16)
    modulated = lax.all_gather(local_mod, "sect", axis=1, tiled=True)
    full_weight = lax.all_gather(weight, "sample", axis=0, tiled=True)
    kernel = full_weight.reshape(9, channels, local_ch)
    kernel_f = kernel.astype(jnp.float32)
    shifts = [moved(modulated, row_step, col_step) for row_step, col_step in OFFSETS]
    conv_out = jnp.zeros(features.shape, jnp.float32)
    for index in range(9):
        conv_out = conv_out + jnp.einsum(
            "nip,io->nop", shifts[index], kernel[index], preferred_element_type=jnp.float32
        )
    kernel_sq = jnp.sum(kernel_f * kernel_f, axis=0)
    style_sq = style * style
    energy = jnp.dot(style_sq, kernel_sq, precision=lax.Precision.HIGHEST) + EPSILON
    demod = lax.rsqrt(energy)
    styled = (conv_out * demod[:, :, None] + bias[None, :, None]).astype(jnp.bfloat16)
    adjoint_f = adjoint.astype(jnp.float32)
    scaled_adjoint = (adjoint_f * demod[:, :, None]).astype(jnp.bfloat16)
    demod_grad = jnp.sum(adjoint_f * conv_out, axis=2)
    energy_grad = -0.5 * demod_grad * demod * demod * demod
    coupling = jnp.dot(style_sq.T, energy_grad, precision=lax.Precision.HIGHEST)
    grads = []
    for index in range(9):
        grads.append(
            jnp.einsum(
                "nip,nop->io", shifts[index], scaled_adjoint, preferred_element_type=jnp.float32
            )
            + 2.0 * kernel_f[index] * coupling
        )
    grad_terms = jnp.concatenate(grads, axis=0)
    grad_weight = lax.psum_scatter(grad_terms, ("sample", "dom"), scatter_dimension=0, tiled=True)
    back = jnp.zeros((samples, channels, pixels), jnp.float32)
    for index in range(9):
        row_step, col_step = OFFSETS[index]
        partial_back = jnp.einsum(
            "nop,io->nip", scaled_adjoint, kernel[index], preferred_element_type=jnp.float32
        )
        back = back + moved(partial_back, -row_step, -col_step)
    summed = lax.psum_scatter(back, "sect", scatter_dimension=1, tiled=True)
    grad_features = (summed * own_style[:, :, None]).astype(jnp.bfloat16)
    return (styled, grad_weight, grad_features)


MESH = pl.DeviceIdType.MESH
HIGH = lax.Precision.HIGHEST
F32 = jnp.float32
BF16 = jnp.bfloat16
CH = 512
BLOCK = 128
PIXELS = ROWS * WIDTH
OWN = 1152
HALF = 576


def fits(mesh):
    return mesh.shape["sample"] == 4 and mesh.shape["sect"] == 4 and mesh.shape["dom"] == 2


def moved_rows(array, row_step, col_step):
    if col_step != 0:
        place = lax.broadcasted_iota(jnp.int32, (PIXELS, 1), 0)
        col = jnp.bitwise_and(place, WIDTH - 1) + col_step
        array = jnp.where((col >= 0) & (col < WIDTH), pltpu.roll(array, (-col_step) % PIXELS, 0), 0.0)
    edge = jnp.zeros((WIDTH, array.shape[1]), array.dtype)
    if row_step == 1:
        array = jnp.concatenate([array[WIDTH:], edge], axis=0)
    if row_step == -1:
        array = jnp.concatenate([edge, array[:-WIDTH]], axis=0)
    return array


def column(row):
    return jnp.transpose(jnp.broadcast_to(row, (BLOCK, BLOCK)))[:, 0:1]


def fused_kernel(
    features_h, weight_h, style_h, bias_h, adjoint_h, styled, grad_weight, grad_features,
    features, bias, adjoint, in_s, kern, mod, mod_t, adj, adj_t, grad, given, from_dom, to_sample, from_sample, to_sect, from_sect,
    twice, style_all, energy_out, energy_in, egrad_all,
    style_s, style_r, mod_s, mod_r, w_s, w_r, w2_s, w2_r, en_s, en_r,
    gy_s, gy_r, gz_s, gz_r, bk_s, bk_r, eg_s, eg_r,
):
    s = lax.axis_index("sample")
    c = lax.axis_index("sect")
    d = lax.axis_index("dom")
    other = 1 - d

    def at_sample(k):
        return {"sample": lax.rem(s + k, 4)}

    def at_sect(k):
        return {"sect": lax.rem(c + k, 4)}

    def at_cross(k):
        return {"sample": lax.rem(s + k, 4), "dom": other}

    partner = {"dom": other}

    def remote(src, dst, send, recv, where):
        return pltpu.make_async_remote_copy(
            src_ref=src, dst_ref=dst, send_sem=send, recv_sem=recv, device_id=where, device_id_type=MESH
        )

    style_all_own = style_all.at[0, 0]
    own_rows = pl.ds(pl.multiple_of(s * OWN, OWN), OWN)
    loads = [
        pltpu.make_async_copy(source, target, in_s.at[index])
        for index, (source, target) in enumerate(
            (
                (style_h, style_all_own),
                (features_h.at[0], features),
                (weight_h, kern.at[own_rows]),
                (adjoint_h.at[0], adjoint),
                (bias_h, bias),
            )
        )
    ]
    for load in loads:
        load.start()

    barrier = pltpu.get_barrier_semaphore()
    for k in (1, 2, 3):
        for where in (at_sample(k), at_cross(k), at_sect(k)):
            pl.semaphore_signal(barrier, inc=1, device_id=where, device_id_type=MESH)
    pl.semaphore_signal(barrier, inc=1, device_id=partner, device_id_type=MESH)

    own_channels = pl.ds(pl.multiple_of(c * BLOCK, BLOCK), BLOCK)
    def rows_of(shard, part):
        return pl.ds(pl.multiple_of(shard * OWN + part * HALF, HALF), HALF)

    def along(up, j):
        half = kern.at[rows_of(s - j if up else s + j, d)]
        slot = j if up else 3 + j
        return remote(half, half, w_s.at[slot], w_r.at[slot], at_sample(1 if up else 3))

    def across(up, j):
        half = kern.at[rows_of(s - 1 - j if up else s + 1 + j, d)]
        slot = j if up else 3 + j
        return remote(half, half, w2_s.at[slot], w2_r.at[slot], partner)

    def sends(up, j):
        return (s >= j) & (s < 3) if up else (s <= 3 - j) & (s > 0)

    def gets(up, j):
        return s >= j + 1 if up else s <= 2 - j

    def pass_on(j):
        for up in (True, False):

            @pl.when(gets(up, j))
            def _():
                along(up, j).wait_recv()

            if j < 2:

                @pl.when(sends(up, j + 1))
                def _():
                    along(up, j + 1).start()

            @pl.when(gets(up, j))
            def _():
                across(up, j).start()

    def to_others(array, send, recv):
        peers = [(0, k, at_sample(k)) for k in (1, 2, 3)] + [(1, k, at_cross(k)) for k in range(4)]
        copies = [
            remote(array.at[0, 0], array.at[h, k], send.at[h, k], recv.at[h, k], where) for h, k, where in peers
        ]
        for copy in copies:
            copy.start()
        return copies

    loads[0].wait()
    loads[2].wait()
    pl.semaphore_wait(barrier, 10)

    style_c = to_others(style_all, style_s, style_r)
    for up in (True, False):

        @pl.when(sends(up, 0))
        def _():
            along(up, 0).start()

    loads[1].wait()
    style_col = column(style_all[0, 0, :, own_channels])
    mod[own_channels, :] = (features[...].astype(F32) * style_col).astype(BF16)

    mod_c = [
        remote(mod.at[own_channels], mod.at[own_channels], mod_s.at[k], mod_r.at[k], at_sect(k)) for k in (1, 2, 3)
    ]
    for copy in mod_c:
        copy.start()
    squares = kern[own_rows, :].astype(F32)
    squares = squares * squares
    part = squares[0:CH] + squares[CH : 2 * CH]
    tail = part[0:BLOCK] + squares[2 * CH : OWN]
    twice[0:BLOCK] = tail
    twice[BLOCK:CH] = part[BLOCK:]
    twice[CH : CH + BLOCK] = tail
    twice[CH + BLOCK : 2 * CH] = part[BLOCK:]
    kernel_sq = twice[pl.ds(pl.multiple_of(CH - s * BLOCK, BLOCK), CH), :]

    for copy in style_c[0:3]:
        copy.wait_recv()
    styles = jnp.concatenate([style_all[0, k] for k in range(4)] * 2, axis=0)
    terms = jnp.dot(styles * styles, kernel_sq, precision=HIGH, preferred_element_type=F32)
    for k in range(4):
        energy_out[k] = terms[k : k + 1, :]
    en_c = [
        remote(energy_out.at[k], energy_in.at[k], en_s.at[k], en_r.at[k], at_sample(4 - k)) for k in (1, 2, 3)
    ]
    for copy in en_c:
        copy.start()
    pass_on(0)

    loads[3].wait()
    loads[4].wait()
    adj_t[...] = jnp.transpose(adjoint[...].astype(F32))
    for col_step in (-1, 0, 1):
        by_col = moved_rows(adj_t[...], 0, -col_step)
        for row_step in (-1, 0, 1):
            index = OFFSETS.index((row_step, col_step))
            adj[:, index * BLOCK : (index + 1) * BLOCK] = moved_rows(by_col, -row_step, 0).astype(BF16)
    for copy in mod_c:
        copy.wait_recv()
    pass_on(1)

    for index in range(0, 9, 2):
        last = min(index + 2, 9)
        value = jnp.dot(mod[...], adj[:, index * BLOCK : last * BLOCK], preferred_element_type=F32)
        for one in range(index, last):
            grad[one * CH : (one + 1) * CH, :] = value[:, (one - index) * BLOCK : (one - index + 1) * BLOCK]
    energy = energy_out[0] + EPSILON
    for k in (1, 2, 3):
        en_c[k - 1].wait_recv()
        energy = energy + energy_in[k]
    demod = lax.rsqrt(energy)

    def kept(k):
        return grad[rows_of(lax.rem(s + k, 4), d), :] * demod

    def give(k):
        given[k] = (grad[rows_of(lax.rem(s + k, 4), other), :] * demod).astype(BF16)
        copy = remote(given.at[k], from_dom.at[k], gy_s.at[k], gy_r.at[k], partner)
        copy.start()
        return copy

    def hand_on(k):
        gy_c[k].wait_recv()
        to_sample[k] = (kept(k) + from_dom[k].astype(F32)).astype(BF16)
        copy = remote(to_sample.at[k], from_sample.at[k], gz_s.at[k], gz_r.at[k], at_sample(k))
        copy.start()
        return copy

    gy_c = {2: give(2), 1: give(1)}
    pass_on(2)
    gy_c[3] = give(3)
    gy_c[0] = give(0)
    mod_t[...] = jnp.transpose(mod[...])
    for index in range(9):
        part = slice(index * BLOCK, (index + 1) * BLOCK)
        adj[:, part] = (adj[:, part].astype(F32) * demod).astype(BF16)
    gz_c = [hand_on(2), hand_on(1)]
    for j in range(3):
        for up in (True, False):

            @pl.when(gets(up, j))
            def _():
                across(up, j).wait_recv()

    wide = adj[...]

    def back_of(block):
        rows = [
            kern[pl.ds(pl.multiple_of(index * CH + block * BLOCK, BLOCK), BLOCK), :] for index in range(9)
        ]
        return lax.dot_general(
            jnp.concatenate(rows, axis=1), wide, (((1,), (1,)), ((), ())), preferred_element_type=F32
        )

    bk_c = []
    for k in (2, 1, 3):
        to_sect[k] = back_of(lax.rem(c + k, 4)).astype(BF16)
        copy = remote(to_sect.at[k], from_sect.at[k], bk_s.at[k], bk_r.at[k], at_sect(k))
        copy.start()
        bk_c.append(copy)

    gz_c.append(hand_on(3))
    conv_t = jnp.zeros((PIXELS, BLOCK), F32)
    for col_step in (-1, 0, 1):
        three = [OFFSETS.index((row_step, col_step)) * CH for row_step in (-1, 0, 1)]
        value = jnp.dot(
            mod_t[...],
            jnp.concatenate([kern[row : row + CH, :] for row in three], axis=1),
            preferred_element_type=F32,
        )
        by_row = value[:, BLOCK : 2 * BLOCK]
        by_row = by_row + moved_rows(value[:, 0:BLOCK], -1, 0) + moved_rows(value[:, 2 * BLOCK :], 1, 0)
        conv_t = conv_t + moved_rows(by_row, 0, col_step)
    demod_grad = jnp.sum(adj_t[...] * conv_t, axis=0, keepdims=True)
    egrad_all[0, 0] = -0.5 * demod_grad * demod * demod * demod
    eg_c = to_others(egrad_all, eg_s, eg_r)
    styled[0] = jnp.transpose(conv_t * demod + bias[...]).astype(BF16)
    own_back = back_of(c)
    for copy in style_c[3:] + eg_c:
        copy.wait_recv()
    styles = jnp.concatenate([style_all[h, k] for h in range(2) for k in range(4)], axis=0)
    egrads = jnp.concatenate([egrad_all[h, k] for h in range(2) for k in range(4)], axis=0)
    coupling = lax.dot_general(
        styles * styles, egrads, (((0,), (0,)), ((), ())), precision=HIGH, preferred_element_type=F32
    )
    twice[0:CH] = coupling
    twice[CH : 2 * CH] = coupling
    first = pl.multiple_of((2 * s + d) * (HALF - CH), HALF - CH)
    owned = kern[rows_of(s, d), :].astype(F32)
    summed = own_back
    for k, copy in zip((2, 1, 3), bk_c):
        copy.wait_recv()
        summed = summed + from_sect[k].astype(F32)
    grad_features[0] = (summed * style_col).astype(BF16)

    gy_c[0].wait_recv()
    total = kept(0) + from_dom[0].astype(F32)
    for k, copy in zip((2, 1, 3), gz_c):
        copy.wait_recv()
        total = total + from_sample[k].astype(F32)

    grad_weight[...] = total + 2.0 * owned * twice[pl.ds(first, HALF), :]

    for copy in style_c + mod_c + en_c + list(gy_c.values()) + gz_c + bk_c + eg_c:
        copy.wait_send()
    for j in range(3):
        for up in (True, False):

            @pl.when(sends(up, j))
            def _():
                along(up, j).wait_send()

            @pl.when(gets(up, j))
            def _():
                across(up, j).wait_send()


def fused(features, weight, style, bias, adjoint):
    vmem = pl.BlockSpec(memory_space=pltpu.VMEM)
    dma = pltpu.SemaphoreType.DMA((6,))
    by_dom = pltpu.SemaphoreType.DMA((2, 4))
    return tuple(
        pl.pallas_call(
            fused_kernel,
            out_shape=(
                pltpu.VMEM(features.shape, BF16),
                pltpu.VMEM((HALF, BLOCK), F32),
                pltpu.VMEM(features.shape, BF16),
            ),
            in_specs=[pl.BlockSpec(memory_space=pltpu.HBM)] * 5,
            out_specs=(vmem,) * 3,
            scratch_shapes=[
                pltpu.VMEM((BLOCK, PIXELS), BF16),
                pltpu.VMEM((1, BLOCK), F32),
                pltpu.VMEM((BLOCK, PIXELS), BF16),
                pltpu.SemaphoreType.DMA((5,)),
                pltpu.VMEM((9 * CH, BLOCK), BF16),
                pltpu.VMEM((CH, PIXELS), BF16),
                pltpu.VMEM((PIXELS, CH), BF16),
                pltpu.VMEM((PIXELS, 9 * BLOCK), BF16),
                pltpu.VMEM((PIXELS, BLOCK), F32),
                pltpu.VMEM((9 * CH, BLOCK), F32),
                pltpu.VMEM((4, HALF, BLOCK), BF16),
                pltpu.VMEM((4, HALF, BLOCK), BF16),
                pltpu.VMEM((4, HALF, BLOCK), BF16),
                pltpu.VMEM((4, HALF, BLOCK), BF16),
                pltpu.VMEM((4, BLOCK, PIXELS), BF16),
                pltpu.VMEM((4, BLOCK, PIXELS), BF16),
                pltpu.VMEM((2 * CH, BLOCK), F32),
                pltpu.VMEM((2, 4, 1, CH), F32),
                pltpu.VMEM((4, 1, BLOCK), F32),
                pltpu.VMEM((4, 1, BLOCK), F32),
                pltpu.VMEM((2, 4, 1, BLOCK), F32),
            ]
            + [by_dom] * 2 + [dma] * 14 + [by_dom] * 2,
            compiler_params=pltpu.CompilerParams(
                collective_id=0, has_side_effects=True, vmem_limit_bytes=66478080
            ),
        )(features, weight, style, bias.reshape(1, BLOCK), adjoint)
    )


def solution(mesh):
    in_specs = (
        P(("sample", "dom"), "sect", None),
        P("sample", "sect"),
        P(("sample", "dom"), None),
        P("sect"),
        P(("sample", "dom"), "sect", None),
    )
    out_specs = (
        P(("sample", "dom"), "sect", None),
        P(("sample", "dom"), "sect"),
        P(("sample", "dom"), "sect", None),
    )
    body = fused if fits(mesh) else per_device
    return jax.shard_map(
        body, mesh=mesh, in_specs=in_specs, out_specs=out_specs, check_vma=False
    )
```
